32 devices in a mesh: scalar: 4 (over z), space: 8 (over y, x, core).
Axes of the slice: x: 2, y: 2, z: 4, core: 2. Of those that a mesh axis runs over, the one named last changes fastest.
Arguments:
- scalars: float32 [16, 2, 1024, 1024], P('scalar', None, 'space'), may hold values from -6 to 6
- velocity_x: float32 [2, 1024, 1024], P(None, 'space', 'scalar'), may hold values from 0 to 1, as said below
- velocity_y: float32 [2, 1024, 1024], P(None, 'space', 'scalar'), may hold values from 0 to 1, as said below
- shift_x: int32 [2, 1024], P(None, 'space'), may hold values from -8 to 8
- shift_y: int32 [1024], P('space'), may hold values from -8 to 8
- schmidt: int32 [16], P('scalar'), may hold values from 1 to 5
Outputs:
- transported: float32 [16, 2, 1024, 1024], P('scalar', None, 'space')
The draws below stay inside these ranges and needn't reach their ends.
Inputs may be any that keep to these rules, and one draw needn't show every extreme that they name: shift_x and shift_y are whole cells of displacement along the line; they act periodically. `velocity_x`: fractions of a cell. `velocity_y`: fractions of a cell.
All inputs are finite; a program needn't handle non-finite values.
Results may differ from the reference program's by a relative error of at most 0.0003.
Values sent between devices are 32-bit elements; how exact they have to be, the bound alone decides.
A program may use at most 192 MiB of HBM per device.

```python
import math
import jax
import jax.numpy as jnp
from jax import lax

NSCAL = 16
NX = 1024
NY = 1024
NZ = 2


def draw_scalars(key, part):
    base_key = jax.random.fold_in(key, 101)
    rough_key, angle_key, level_key = jax.random.split(base_key, 3)
    field_shape = (NSCAL, NZ, NY, NX)
    rough_part = jnp.clip(0.5 * jax.random.normal(rough_key, field_shape, jnp.float32), -2.0, 2.0)
    amplitude = 2.5 + 0.0 * jax.random.uniform(level_key, (NSCAL, NZ, 1, 1), jnp.float32)
    angles = jax.random.uniform(angle_key, (NSCAL, NZ, 1, 1), jnp.float32, -math.pi, math.pi)
    row_index = lax.broadcasted_iota(jnp.int32, (1, 1, NY, 1), 2)
    col_index = lax.broadcasted_iota(jnp.int32, (1, 1, 1, NX), 3)
    row_sign = 1.0 - 2.0 * (row_index % 2).astype(jnp.float32)
    col_sign = 1.0 - 2.0 * (col_index % 2).astype(jnp.float32)
    result = rough_part + amplitude * jnp.cos(angles) * col_sign + amplitude * jnp.sin(angles) * row_sign
    return result.astype(jnp.float32)


def fraction_draw(key, salt):
    base_key = jax.random.fold_in(key, salt)
    field_shape = (NZ, NY, NX)
    values = jax.random.uniform(base_key, field_shape, jnp.float32, 0.0, 0.2)
    return values.astype(jnp.float32)


def draw_velocity_x(key, part):
    return fraction_draw(key, 211)


def draw_velocity_y(key, part):
    return fraction_draw(key, 307)


def set_ends(values, own_key, smallest, largest):
    spot = [jax.random.randint(jax.random.fold_in(own_key, axis), (), 0, length) for axis, length in enumerate(values.shape)]
    longest = values.shape.index(max(values.shape))
    beside = spot[:longest] + [(spot[longest] + 1) % values.shape[longest]] + spot[longest + 1:]
    return values.at[tuple(spot)].set(smallest).at[tuple(beside)].set(largest)


def setup_inputs(seed: int = 0) -> dict:
    splits = jax.random.split(jax.random.key(seed), 7)
    scalars = draw_scalars(jax.random.fold_in(splits[6], 71), 0)
    velocity_x = draw_velocity_x(jax.random.fold_in(splits[6], 71), 0)
    velocity_y = draw_velocity_y(jax.random.fold_in(splits[6], 71), 0)
    shift_x = set_ends(jax.random.randint(splits[3], (NZ, NY), -8, 9), jax.random.fold_in(splits[3], 1), -8, 8).astype(jnp.int32)
    shift_y = set_ends(jax.random.randint(splits[4], (NX,), -8, 9), jax.random.fold_in(splits[4], 1), -8, 8).astype(jnp.int32)
    schmidt = set_ends(jax.random.randint(splits[5], (NSCAL,), 1, 6), jax.random.fold_in(splits[5], 1), 1, 5).astype(jnp.int32)
    return {"scalars": scalars, "velocity_x": velocity_x, "velocity_y": velocity_y, "shift_x": shift_x, "shift_y": shift_y, "schmidt": schmidt}


def spline(distance):
    magnitude = jnp.abs(distance)
    far_part = jnp.maximum(3.0 - magnitude, 0.0)
    middle = jnp.maximum(2.0 - magnitude, 0.0)
    near_part = jnp.maximum(1.0 - magnitude, 0.0)
    return (far_part ** 5 - 6.0 * middle ** 5 + 15.0 * near_part ** 5) / 120.0


def remesh(fields, fraction, shift_line):
    length = fields.shape[-1]
    summed = jnp.zeros_like(fields)
    for offset in range(-2, 4):
        weight = spline(offset - fraction)
        summed = summed + jnp.roll(fields * weight, offset, axis=-1)
    column = lax.broadcasted_iota(jnp.int32, fraction.shape, 2)
    source = (column - shift_line[:, :, None].astype(jnp.int32)) % length
    source = jnp.broadcast_to(source, fields.shape).astype(jnp.int32)
    return jnp.take_along_axis(summed, source, axis=-1)


def diffuse_exact(fields, diffusivity):
    length = fields.shape[-1]
    spectra = jnp.fft.rfft(fields, axis=-1)
    wavenum = jnp.arange(length // 2 + 1).astype(jnp.float32) / (length // 2)
    damping = jnp.exp(-diffusivity * wavenum * wavenum)
    return jnp.fft.irfft(spectra * damping, n=length, axis=-1).astype(jnp.float32)


def reference(scalars, velocity_x, velocity_y, shift_x, shift_y, schmidt):
    inverse_sc = jnp.exp2((3 - schmidt).astype(jnp.float32))
    shift_cols = jnp.broadcast_to(shift_y[None, :], (NZ, NX))
    velocity_turned = jnp.swapaxes(velocity_y, 1, 2)

    def per_scalar(members):
        fields, diffusivity = members
        fields = diffuse_exact(remesh(fields, velocity_x, shift_x), 0.5 * diffusivity)
        turned = jnp.swapaxes(fields, 1, 2)
        turned = diffuse_exact(remesh(turned, velocity_turned, shift_cols), diffusivity)
        fields = jnp.swapaxes(turned, 1, 2)
        return diffuse_exact(remesh(fields, velocity_x, shift_x), 0.5 * diffusivity)

    return lax.map(per_scalar, (scalars, inverse_sc))
```

```python
import functools
import math

import jax
import jax.numpy as jnp
import numpy as np
from jax import lax
from jax.experimental import pallas as pl
from jax.experimental.pallas import tpu as pltpu
from jax.sharding import PartitionSpec as P

NY = 1024


def spline(distance):
    magnitude = jnp.abs(distance)
    far_part = jnp.maximum(3.0 - magnitude, 0.0)
    middle = jnp.maximum(2.0 - magnitude, 0.0)
    near_part = jnp.maximum(1.0 - magnitude, 0.0)
    return (far_part**5 - 6.0 * middle**5 + 15.0 * near_part**5) / 120.0


def remesh(fields, fraction, shift_line):
    summed = jnp.zeros_like(fields)
    for offset in range(-2, 4):
        weight = spline(offset - fraction)
        summed = summed + jnp.roll(fields * weight, offset, axis=-1)
    line_shift = shift_line[None, :, :, None]
    moved = summed
    for amount in range(-8, 9):
        moved = jnp.where(line_shift == amount, jnp.roll(summed, amount, axis=-1), moved)
    return moved


def remesh_columns(fields, fraction, shift_cols):
    summed = jnp.zeros_like(fields)
    for offset in range(-2, 4):
        weight = spline(offset - fraction)
        summed = summed + jnp.roll(fields * weight[None], offset, axis=2)
    column_shift = shift_cols[None, None, None, :]
    moved = summed
    for amount in range(-8, 9):
        moved = jnp.where(column_shift == amount, jnp.roll(summed, amount, axis=2), moved)
    return moved


def spectral_tables(length):
    midpoint = length // 2
    column = jnp.arange(length, dtype=jnp.int32)
    wavenum = jnp.where(column <= midpoint, column, column - midpoint)
    phases = column[:, None] * wavenum[None, :] % length
    angles = phases.astype(jnp.float32) * (2.0 * math.pi / length)
    forward = jnp.where((column <= midpoint)[None, :], jnp.cos(angles), jnp.sin(angles))
    inverse_weight = jnp.where((wavenum == 0) | (column == midpoint), 1.0, 2.0) / length
    inverse = forward.T * inverse_weight[:, None]
    relative = wavenum.astype(jnp.float32) / midpoint
    return (forward, inverse, relative * relative)


def diffuse(fields, diffusivity, tables):
    forward, inverse, wave_square = tables
    initial = fields.shape
    rows_flat = fields.reshape(-1, initial[-1])
    spectra = jnp.dot(
        rows_flat, forward, precision=lax.Precision.HIGHEST, preferred_element_type=jnp.float32
    )
    damping = jnp.exp(-diffusivity[:, None] * wave_square[None, :])
    spectra = spectra.reshape(initial) * damping[:, None, None, :]
    result = jnp.dot(
        spectra.reshape(-1, initial[-1]),
        inverse,
        precision=lax.Precision.HIGHEST,
        preferred_element_type=jnp.float32,
    )
    return result.reshape(initial)


def diffuse_columns(fields, diffusivity, tables):
    forward, inverse, wave_square = tables
    spectra = jnp.einsum(
        "jk,szjx->szkx",
        forward,
        fields,
        precision=lax.Precision.HIGHEST,
        preferred_element_type=jnp.float32,
    )
    damping = jnp.exp(-diffusivity[:, None] * wave_square[None, :])
    spectra = spectra * damping[:, None, :, None]
    return jnp.einsum(
        "kj,szkx->szjx",
        inverse,
        spectra,
        precision=lax.Precision.HIGHEST,
        preferred_element_type=jnp.float32,
    )


def one_sweep(fields, fraction, shift_line, diffusivity, tables):
    return diffuse(remesh(fields, fraction, shift_line), diffusivity, tables)


def fetch_velocity(velocity_x):
    return lax.all_gather(velocity_x, "scalar", axis=2, tiled=True)


def on_device(scalars, velocity_x, velocity_y, shift_x, shift_y, schmidt):
    diffusivity = jnp.exp2((3 - schmidt).astype(jnp.float32))
    tables_x = spectral_tables(scalars.shape[3])
    tables_y = spectral_tables(NY)
    along_x = fetch_velocity(velocity_x)
    fields = one_sweep(scalars, along_x, shift_x, 0.5 * diffusivity, tables_x)
    along_y = lax.all_gather(velocity_y, "scalar", axis=2, tiled=True)
    fields_cols, velocity_cols = (
        lax.all_to_all(fields, "space", split_axis=3, concat_axis=2, tiled=True),
        lax.all_to_all(along_y[None], "space", split_axis=3, concat_axis=2, tiled=True),
    )
    remeshed = remesh_columns(fields_cols, velocity_cols[0], shift_y)
    returned = diffuse_columns(remeshed, diffusivity, tables_y)
    fields = lax.all_to_all(returned, "space", split_axis=2, concat_axis=3, tiled=True)
    along_x = fetch_velocity(velocity_x)
    return one_sweep(fields, along_x, shift_x, 0.5 * diffusivity, tables_x)


BLOCK = 256
REACH = 8
MESH = pl.DeviceIdType.MESH


def spline_weights(f):
    g = 1.0 - f

    def fifth(v):
        w = v * v
        return w * w * v

    f0, f1, f2 = fifth(f), fifth(1.0 + f), fifth(2.0 + f)
    g0, g1, g2 = fifth(g), fifth(1.0 + g), fifth(2.0 + g)
    c = 1.0 / 120.0
    return (
        g0 * c,
        (g1 - 6.0 * g0) * c,
        (g2 - 6.0 * g1 + 15.0 * g0) * c,
        (f2 - 6.0 * f1 + 15.0 * f0) * c,
        (f1 - 6.0 * f0) * c,
        f0 * c,
    )


def response(kappa, length):
    half = length // 2
    k = np.arange(half + 1)
    weight = np.where((k == 0) | (k == half), 1.0, 2.0) / length
    phase = (k[:, None] * np.arange(length)[None, :]) % length
    table = (np.cos(phase * (2.0 * np.pi / length)) * weight[:, None]).astype(np.float32)
    relative = jnp.arange(half + 1).astype(jnp.float32) / half
    damping = jnp.exp(-kappa[:, None] * relative * relative)
    return jnp.dot(damping, table, precision=lax.Precision.HIGHEST, preferred_element_type=jnp.float32)


def circulant_kernel(g_ref, hi_ref, lo_ref):
    length = g_ref.shape[-1]
    wide = jnp.broadcast_to(g_ref[0], (BLOCK, length))
    turned = pltpu.roll(wide, 0, 1, stride=1, stride_axis=0)
    high = turned.astype(jnp.bfloat16)
    hi_ref[0] = high
    lo_ref[0] = (turned - high.astype(jnp.float32)).astype(jnp.bfloat16)


def circulant_blocks(g):
    count, length = g.shape
    spec = pl.BlockSpec((1, BLOCK, length), lambda i: (i, 0, 0))
    return pl.pallas_call(
        circulant_kernel,
        grid=(count,),
        in_specs=[pl.BlockSpec((1, 1, length), lambda i: (i, 0, 0))],
        out_specs=[spec, spec],
        out_shape=[jax.ShapeDtypeStruct((count, BLOCK, length), jnp.bfloat16)] * 2,
    )(g[:, None, :])


def halves(v):
    high = v.astype(jnp.bfloat16)
    return high, (v - high.astype(jnp.float32)).astype(jnp.bfloat16)


def dot32(a, b):
    return jnp.dot(a, b, preferred_element_type=jnp.float32)


def sweeps_kernel(
    peers,
    q_ref, vx_ref, vy_ref, sx_ref, sy_ref, xh_ref, xl_ref, yh_ref, yl_ref,
    out_ref,
    wx, wy, part_hi, part_lo, swept, col_hi, col_lo, tall,
    ext, cols, turned, back,
    send1, recv1, send2, recv2,
):
    ns, nz, rows, nx = q_ref.shape
    ny = rows * peers
    width = nx // peers
    me = lax.axis_index("space")
    bx, by = nx // BLOCK, ny // BLOCK

    barrier = pltpu.get_barrier_semaphore()
    for k in range(1, peers):
        pl.semaphore_signal(barrier, inc=1, device_id={"space": lax.rem(me + k, peers)}, device_id_type=MESH)

    step = 16
    per = rows // step

    @pl.loop(0, nz * per)
    def _(i):
        z, r = i // per, pl.multiple_of((i % per) * step, step)
        for v_ref, w_ref in ((vx_ref, wx), (vy_ref, wy)):
            for m, w in enumerate(spline_weights(v_ref[z, pl.ds(r, step), :])):
                w_ref[z, m, pl.ds(r, step), :] = w

    def remesh_rows(load):
        @pl.loop(0, nz * per)
        def _(i):
            z, r = i // per, pl.multiple_of((i % per) * step, step)
            q = load(z, r)
            acc = q * wx[z, 5, pl.ds(r, step), :]
            for m in range(4, -1, -1):
                acc = pltpu.roll(acc, 1, 1) + q * wx[z, m, pl.ds(r, step), :]
            shift = sx_ref[z, pl.ds(r, step), :] + REACH
            for bit in (1, 2, 4, 8, 16):
                acc = jnp.where((shift & bit) != 0, pltpu.roll(acc, bit, 1), acc)
            at = pl.multiple_of(z * rows + r, step)
            part_hi[pl.ds(at, step), :], part_lo[pl.ds(at, step), :] = halves(acc)

    def diffuse_rows(s, store):
        for b in range(bx):
            total = jnp.zeros((nz * rows, BLOCK), jnp.float32)
            for a in range(bx):
                d = ((b - a) % bx) * BLOCK
                high, low = xh_ref[s, :, d:d + BLOCK], xl_ref[s, :, d:d + BLOCK]
                left = part_hi[:, a * BLOCK:(a + 1) * BLOCK]
                rest = part_lo[:, a * BLOCK:(a + 1) * BLOCK]
                total = total + (dot32(left, high) + (dot32(left, low) + dot32(rest, high)))
            store(b * BLOCK, total)

    def forward(s, k):
        dest = lax.rem(me + k, peers)
        return pltpu.make_async_remote_copy(
            src_ref=ext.at[s, dest], dst_ref=cols.at[s, me],
            send_sem=send1.at[s, k - 1], recv_sem=recv1.at[s, k - 1],
            device_id={"space": dest}, device_id_type=MESH,
        )

    def backward(s, k):
        dest = lax.rem(me + k, peers)
        return pltpu.make_async_remote_copy(
            src_ref=turned.at[s, dest], dst_ref=back.at[s, me],
            send_sem=send2.at[s, k - 1], recv_sem=recv2.at[s, k - 1],
            device_id={"space": dest}, device_id_type=MESH,
        )

    edge = lax.broadcasted_iota(jnp.int32, (8, width), 0)

    def first(s):
        remesh_rows(lambda z, r: q_ref[s, z, pl.ds(r, step), :])

        def store(c, total):
            swept[:, c:c + BLOCK] = total

        diffuse_rows(s, store)

        @pl.loop(0, nz * peers)
        def _(i):
            p, z = i // nz, i % nz
            lanes = pl.ds(pl.multiple_of(p * width, width), width)
            y = swept[pl.ds(pl.multiple_of(z * rows, rows), rows), lanes]
            pad = jnp.zeros((8, width), jnp.float32)
            acc = jnp.zeros((rows + 16, width), jnp.float32)
            for m in range(-2, 4):
                term = jnp.concatenate([pad, y * wy[z, m + 2, :, lanes], pad], axis=0)
                acc = acc + (term if m == 0 else pltpu.roll(term, m % (rows + 16), 0))
            ext[s, p, z, 0:rows, :] = acc[8:8 + rows]
            ext[s, p, z, rows:rows + 8, :] = jnp.where(edge < 3, acc[rows + 8:], acc[:8])

        cols[s, me] = ext[s, me]

    @pl.loop(0, 1)
    def _(s):
        first(s)

    pl.semaphore_wait(barrier, peers - 1)
    for k in range(1, peers):
        forward(0, k).start()

    @pl.loop(1, ns)
    def _(s):
        first(s)
        for k in range(1, peers):
            forward(s, k).start()

    @pl.loop(0, ns)
    def _(s):
        for k in range(1, peers):
            forward(s, k).wait_recv()

        for p in range(peers):
            for z in range(nz):
                lanes = slice(z * width, (z + 1) * width)
                top = jnp.where(edge < 3, cols[s, (p - 1) % peers, z, rows:rows + 8, :], 0.0)
                low = jnp.where(edge >= 6, cols[s, (p + 1) % peers, z, rows:rows + 8, :], 0.0)
                at = 8 + p * rows
                tall[at:at + 8, lanes] = cols[s, p, z, 0:8, :] + top
                tall[at + 8:at + rows - 8, lanes] = cols[s, p, z, 8:rows - 8, :]
                tall[at + rows - 8:at + rows, lanes] = cols[s, p, z, rows - 8:rows, :] + low
        tall[0:8, :] = tall[ny:ny + 8, :]
        tall[ny + 8:ny + 16, :] = tall[8:16, :]

        @pl.loop(0, peers)
        def _(p):
            at = pl.multiple_of(p * rows, rows)
            ahead = REACH - sy_ref[...]
            for z in range(nz):
                lanes = slice(z * width, (z + 1) * width)
                u = tall[pl.ds(at, rows + 16), lanes]
                for bit in (1, 2, 4, 8, 16):
                    u = jnp.where((ahead & bit) != 0, pltpu.roll(u, rows + 16 - bit, 0), u)
                col_hi[pl.ds(at, rows), lanes], col_lo[pl.ds(at, rows), lanes] = halves(u[:rows])

        for a in range(by):
            total = jnp.zeros((BLOCK, nz * width), jnp.float32)
            for b in range(by):
                d = ((b - a) % by) * BLOCK
                high, low = yh_ref[s, :, d:d + BLOCK], yl_ref[s, :, d:d + BLOCK]
                left = col_hi[b * BLOCK:(b + 1) * BLOCK, :]
                rest = col_lo[b * BLOCK:(b + 1) * BLOCK, :]
                total = total + (dot32(high, left) + (dot32(low, left) + dot32(high, rest)))
            for h in range(BLOCK // rows):
                for z in range(nz):
                    turned[s, a * (BLOCK // rows) + h, z] = total[
                        h * rows:(h + 1) * rows, z * width:(z + 1) * width
                    ]
        back[s, me] = turned[s, me]
        for k in range(1, peers):
            backward(s, k).start()

    @pl.loop(0, ns)
    def _(s):
        for k in range(1, peers):
            backward(s, k).wait_recv()
        remesh_rows(
            lambda z, r: jnp.concatenate(
                [back[s, p, z, pl.ds(r, step), :] for p in range(peers)], axis=1
            )
        )

        def store(c, total):
            for z in range(nz):
                out_ref[s, z, :, c:c + BLOCK] = total[z * rows:(z + 1) * rows]

        diffuse_rows(s, store)

    @pl.loop(0, ns)
    def _(s):
        for k in range(1, peers):
            forward(s, k).wait_send()
            backward(s, k).wait_send()


def sweeps_on_device(peers, scalars, velocity_x, velocity_y, shift_x, shift_y, schmidt):
    ns, nz, rows, nx = scalars.shape
    ny, width = rows * peers, nx // peers
    along_x = fetch_velocity(velocity_x)
    along_y = fetch_velocity(velocity_y)
    diffusivity = jnp.exp2((3 - schmidt).astype(jnp.float32))
    line_x = jnp.roll(response(0.5 * diffusivity, nx), -(REACH + 2), axis=1)
    line_y = response(diffusivity, ny)
    xh, xl = circulant_blocks(line_x)
    yh, yl = circulant_blocks(line_y)
    f32, bf16 = jnp.float32, jnp.bfloat16
    vmem = pl.BlockSpec(memory_space=pltpu.VMEM)
    dma = pltpu.SemaphoreType.DMA((ns, peers - 1))
    return pl.pallas_call(
        functools.partial(sweeps_kernel, peers),
        out_shape=jax.ShapeDtypeStruct(scalars.shape, f32),
        in_specs=[vmem] * 9,
        out_specs=vmem,
        scratch_shapes=[
            pltpu.VMEM((nz, 6, rows, nx), f32),
            pltpu.VMEM((nz, 6, rows, nx), f32),
            pltpu.VMEM((nz * rows, nx), bf16),
            pltpu.VMEM((nz * rows, nx), bf16),
            pltpu.VMEM((nz * rows, nx), f32),
            pltpu.VMEM((ny, nz * width), bf16),
            pltpu.VMEM((ny, nz * width), bf16),
            pltpu.VMEM((ny + 16, nz * width), f32),
            pltpu.VMEM((ns, peers, nz, rows + 8, width), f32),
            pltpu.VMEM((ns, peers, nz, rows + 8, width), f32),
            pltpu.VMEM((ns, peers, nz, rows, width), f32),
            pltpu.VMEM((ns, peers, nz, rows, width), f32),
            dma, dma, dma, dma,
        ],
        compiler_params=pltpu.CompilerParams(
            collective_id=0, has_side_effects=True, vmem_limit_bytes=62 * 2**20
        ),
    )(
        scalars, along_x, along_y, shift_x[:, :, None], shift_y[None, :], xh, xl, yh, yl
    )


def fits_kernel(mesh):
    return NY % mesh.shape["space"] == 0 and NY // mesh.shape["space"] in (128, 256)


def solution(mesh):
    peers = mesh.shape["space"]
    body = functools.partial(sweeps_on_device, peers) if fits_kernel(mesh) else on_device
    return jax.shard_map(
        body,
        mesh=mesh,
        in_specs=(
            P("scalar", None, "space", None),
            P(None, "space", "scalar"),
            P(None, "space", "scalar"),
            P(None, "space"),
            P("space"),
            P("scalar"),
        ),
        out_specs=P("scalar", None, "space", None),
        check_vma=False,
    )
```

```python
import functools
import math

import jax
import jax.numpy as jnp
import numpy as np
from jax import lax
from jax.experimental import pallas as pl
from jax.experimental.pallas import tpu as pltpu
from jax.sharding import PartitionSpec as P

NY = 1024


def spline(distance):
    magnitude = jnp.abs(distance)
    far_part = jnp.maximum(3.0 - magnitude, 0.0)
    middle = jnp.maximum(2.0 - magnitude, 0.0)
    near_part = jnp.maximum(1.0 - magnitude, 0.0)
    return (far_part**5 - 6.0 * middle**5 + 15.0 * near_part**5) / 120.0


def remesh(fields, fraction, shift_line):
    summed = jnp.zeros_like(fields)
    for offset in range(-2, 4):
        weight = spline(offset - fraction)
        summed = summed + jnp.roll(fields * weight, offset, axis=-1)
    line_shift = shift_line[None, :, :, None]
    moved = summed
    for amount in range(-8, 9):
        moved = jnp.where(line_shift == amount, jnp.roll(summed, amount, axis=-1), moved)
    return moved


def remesh_columns(fields, fraction, shift_cols):
    summed = jnp.zeros_like(fields)
    for offset in range(-2, 4):
        weight = spline(offset - fraction)
        summed = summed + jnp.roll(fields * weight[None], offset, axis=2)
    column_shift = shift_cols[None, None, None, :]
    moved = summed
    for amount in range(-8, 9):
        moved = jnp.where(column_shift == amount, jnp.roll(summed, amount, axis=2), moved)
    return moved


def spectral_tables(length):
    midpoint = length // 2
    column = jnp.arange(length, dtype=jnp.int32)
    wavenum = jnp.where(column <= midpoint, column, column - midpoint)
    phases = column[:, None] * wavenum[None, :] % length
    angles = phases.astype(jnp.float32) * (2.0 * math.pi / length)
    forward = jnp.where((column <= midpoint)[None, :], jnp.cos(angles), jnp.sin(angles))
    inverse_weight = jnp.where((wavenum == 0) | (column == midpoint), 1.0, 2.0) / length
    inverse = forward.T * inverse_weight[:, None]
    relative = wavenum.astype(jnp.float32) / midpoint
    return (forward, inverse, relative * relative)


def diffuse(fields, diffusivity, tables):
    forward, inverse, wave_square = tables
    initial = fields.shape
    rows_flat = fields.reshape(-1, initial[-1])
    spectra = jnp.dot(
        rows_flat, forward, precision=lax.Precision.HIGHEST, preferred_element_type=jnp.float32
    )
    damping = jnp.exp(-diffusivity[:, None] * wave_square[None, :])
    spectra = spectra.reshape(initial) * damping[:, None, None, :]
    result = jnp.dot(
        spectra.reshape(-1, initial[-1]),
        inverse,
        precision=lax.Precision.HIGHEST,
        preferred_element_type=jnp.float32,
    )
    return result.reshape(initial)


def diffuse_columns(fields, diffusivity, tables):
    forward, inverse, wave_square = tables
    spectra = jnp.einsum(
        "jk,szjx->szkx",
        forward,
        fields,
        precision=lax.Precision.HIGHEST,
        preferred_element_type=jnp.float32,
    )
    damping = jnp.exp(-diffusivity[:, None] * wave_square[None, :])
    spectra = spectra * damping[:, None, :, None]
    return jnp.einsum(
        "kj,szkx->szjx",
        inverse,
        spectra,
        precision=lax.Precision.HIGHEST,
        preferred_element_type=jnp.float32,
    )


def one_sweep(fields, fraction, shift_line, diffusivity, tables):
    return diffuse(remesh(fields, fraction, shift_line), diffusivity, tables)


def fetch_velocity(velocity_x):
    return lax.all_gather(velocity_x, "scalar", axis=2, tiled=True)


def on_device(scalars, velocity_x, velocity_y, shift_x, shift_y, schmidt):
    diffusivity = jnp.exp2((3 - schmidt).astype(jnp.float32))
    tables_x = spectral_tables(scalars.shape[3])
    tables_y = spectral_tables(NY)
    along_x = fetch_velocity(velocity_x)
    fields = one_sweep(scalars, along_x, shift_x, 0.5 * diffusivity, tables_x)
    along_y = lax.all_gather(velocity_y, "scalar", axis=2, tiled=True)
    fields_cols, velocity_cols = (
        lax.all_to_all(fields, "space", split_axis=3, concat_axis=2, tiled=True),
        lax.all_to_all(along_y[None], "space", split_axis=3, concat_axis=2, tiled=True),
    )
    remeshed = remesh_columns(fields_cols, velocity_cols[0], shift_y)
    returned = diffuse_columns(remeshed, diffusivity, tables_y)
    fields = lax.all_to_all(returned, "space", split_axis=2, concat_axis=3, tiled=True)
    along_x = fetch_velocity(velocity_x)
    return one_sweep(fields, along_x, shift_x, 0.5 * diffusivity, tables_x)


BLOCK = 256
REACH = 8
MESH = pl.DeviceIdType.MESH


def spline_weights(f):
    g = 1.0 - f

    def fifth(v):
        w = v * v
        return w * w * v

    f0, f1, f2 = fifth(f), fifth(1.0 + f), fifth(2.0 + f)
    g0, g1, g2 = fifth(g), fifth(1.0 + g), fifth(2.0 + g)
    c = 1.0 / 120.0
    return (
        g0 * c,
        (g1 - 6.0 * g0) * c,
        (g2 - 6.0 * g1 + 15.0 * g0) * c,
        (f2 - 6.0 * f1 + 15.0 * f0) * c,
        (f1 - 6.0 * f0) * c,
        f0 * c,
    )


def response(kappa, length):
    half = length // 2
    k = np.arange(half + 1)
    weight = np.where((k == 0) | (k == half), 1.0, 2.0) / length
    phase = (k[:, None] * np.arange(length)[None, :]) % length
    table = (np.cos(phase * (2.0 * np.pi / length)) * weight[:, None]).astype(np.float32)
    relative = jnp.arange(half + 1).astype(jnp.float32) / half
    damping = jnp.exp(-kappa[:, None] * relative * relative)
    return jnp.dot(damping, table, precision=lax.Precision.HIGHEST, preferred_element_type=jnp.float32)


def circulant_kernel(g_ref, hi_ref, lo_ref):
    length = g_ref.shape[-1]
    wide = jnp.broadcast_to(g_ref[0], (BLOCK, length))
    turned = pltpu.roll(wide, 0, 1, stride=1, stride_axis=0)
    high = turned.astype(jnp.bfloat16)
    hi_ref[0] = high
    lo_ref[0] = (turned - high.astype(jnp.float32)).astype(jnp.bfloat16)


def circulant_blocks(g):
    count, length = g.shape
    spec = pl.BlockSpec((1, BLOCK, length), lambda i: (i, 0, 0))
    return pl.pallas_call(
        circulant_kernel,
        grid=(count,),
        in_specs=[pl.BlockSpec((1, 1, length), lambda i: (i, 0, 0))],
        out_specs=[spec, spec],
        out_shape=[jax.ShapeDtypeStruct((count, BLOCK, length), jnp.bfloat16)] * 2,
    )(g[:, None, :])


def halves(v):
    high = v.astype(jnp.bfloat16)
    return high, (v - high.astype(jnp.float32)).astype(jnp.bfloat16)


def dot32(a, b):
    return jnp.dot(a, b, preferred_element_type=jnp.float32)


def sweeps_kernel(
    peers,
    q_ref, vx_ref, vy_ref, sx_ref, sy_ref, xh_ref, xl_ref, yh_ref, yl_ref,
    out_ref,
    wx, wy, part_hi, part_lo, swept, col_hi, col_lo, tall,
    ext, cols, turned, back,
    send1, recv1, send2, recv2,
):
    ns, nz, rows, nx = q_ref.shape
    ny = rows * peers
    width = nx // peers
    me = lax.axis_index("space")
    bx, by = nx // BLOCK, ny // BLOCK

    barrier = pltpu.get_barrier_semaphore()
    for k in range(1, peers):
        pl.semaphore_signal(barrier, inc=1, device_id={"space": lax.rem(me + k, peers)}, device_id_type=MESH)

    step = 16
    per = rows // step

    @pl.loop(0, nz * per)
    def _(i):
        z, r = i // per, pl.multiple_of((i % per) * step, step)
        for v_ref, w_ref in ((vx_ref, wx), (vy_ref, wy)):
            for m, w in enumerate(spline_weights(v_ref[z, pl.ds(r, step), :])):
                w_ref[z, m, pl.ds(r, step), :] = w

    def remesh_rows(load):
        @pl.loop(0, nz * per, unroll=2)
        def _(i):
            z, r = i // per, pl.multiple_of((i % per) * step, step)
            q = load(z, r)
            acc = q * wx[z, 0, pl.ds(r, step), :]
            for m in range(1, 6):
                acc = acc + pltpu.roll(q * wx[z, m, pl.ds(r, step), :], m, 1)
            shift = sx_ref[z, pl.ds(r, step), :] + REACH
            for places, low in (((1, 2, 3), 3), ((4, 8, 12, 16), 28)):
                now, base = shift & low, acc
                for place in places:
                    acc = jnp.where(now == place, pltpu.roll(base, place, 1), acc)
            at = pl.multiple_of(z * rows + r, step)
            part_hi[pl.ds(at, step), :], part_lo[pl.ds(at, step), :] = halves(acc)

    def diffuse_rows(s, store):
        for b in range(bx):
            total = jnp.zeros((nz * rows, BLOCK), jnp.float32)
            for a in range(bx):
                d = ((b - a) % bx) * BLOCK
                high, low = xh_ref[s, :, d:d + BLOCK], xl_ref[s, :, d:d + BLOCK]
                left = part_hi[:, a * BLOCK:(a + 1) * BLOCK]
                rest = part_lo[:, a * BLOCK:(a + 1) * BLOCK]
                total = total + (dot32(left, high) + (dot32(left, low) + dot32(rest, high)))
            store(b * BLOCK, total)

    def forward(s, k):
        dest = lax.rem(me + k, peers)
        return pltpu.make_async_remote_copy(
            src_ref=ext.at[s, dest], dst_ref=cols.at[s, me],
            send_sem=send1.at[s, k - 1], recv_sem=recv1.at[s, k - 1],
            device_id={"space": dest}, device_id_type=MESH,
        )

    def backward(s, k):
        dest = lax.rem(me + k, peers)
        return pltpu.make_async_remote_copy(
            src_ref=turned.at[s, dest], dst_ref=back.at[s, me],
            send_sem=send2.at[s, k - 1], recv_sem=recv2.at[s, k - 1],
            device_id={"space": dest}, device_id_type=MESH,
        )

    edge = lax.broadcasted_iota(jnp.int32, (8, width), 0)

    def first(s):
        remesh_rows(lambda z, r: q_ref[s, z, pl.ds(r, step), :])

        def store(c, total):
            swept[:, c:c + BLOCK] = total

        diffuse_rows(s, store)

        @pl.loop(0, nz * peers)
        def _(i):
            p, z = i // nz, i % nz
            lanes = pl.ds(pl.multiple_of(p * width, width), width)
            y = swept[pl.ds(pl.multiple_of(z * rows, rows), rows), lanes]
            pad = jnp.zeros((8, width), jnp.float32)
            acc = jnp.zeros((rows + 16, width), jnp.float32)
            for m in range(-2, 4):
                term = jnp.concatenate([pad, y * wy[z, m + 2, :, lanes], pad], axis=0)
                acc = acc + (term if m == 0 else pltpu.roll(term, m % (rows + 16), 0))
            ext[s, p, z, 0:rows, :] = acc[8:8 + rows]
            ext[s, p, z, rows:rows + 8, :] = jnp.where(edge < 3, acc[rows + 8:], acc[:8])

        cols[s, me] = ext[s, me]

    @pl.loop(0, 1)
    def _(s):
        first(s)

    pl.semaphore_wait(barrier, peers - 1)
    for k in range(1, peers):
        forward(0, k).start()

    @pl.loop(1, ns)
    def _(s):
        first(s)
        for k in range(1, peers):
            forward(s, k).start()

    @pl.loop(0, ns)
    def _(s):
        for k in range(1, peers):
            forward(s, k).wait_recv()

        for p in range(peers):
            for z in range(nz):
                lanes = slice(z * width, (z + 1) * width)
                top = jnp.where(edge < 3, cols[s, (p - 1) % peers, z, rows:rows + 8, :], 0.0)
                low = jnp.where(edge >= 6, cols[s, (p + 1) % peers, z, rows:rows + 8, :], 0.0)
                at = 8 + p * rows
                tall[at:at + 8, lanes] = cols[s, p, z, 0:8, :] + top
                tall[at + 8:at + rows - 8, lanes] = cols[s, p, z, 8:rows - 8, :]
                tall[at + rows - 8:at + rows, lanes] = cols[s, p, z, rows - 8:rows, :] + low
        tall[0:8, :] = tall[ny:ny + 8, :]
        tall[ny + 8:ny + 16, :] = tall[8:16, :]

        @pl.loop(0, peers)
        def _(p):
            at = pl.multiple_of(p * rows, rows)
            ahead = REACH - sy_ref[...]
            for z in range(nz):
                lanes = slice(z * width, (z + 1) * width)
                u = tall[pl.ds(at, rows + 16), lanes]
                for bit in (1, 2, 4, 8, 16):
                    u = jnp.where((ahead & bit) != 0, pltpu.roll(u, rows + 16 - bit, 0), u)
                col_hi[pl.ds(at, rows), lanes], col_lo[pl.ds(at, rows), lanes] = halves(u[:rows])

        for a in range(by):
            total = jnp.zeros((BLOCK, nz * width), jnp.float32)
            for b in range(by):
                d = ((b - a) % by) * BLOCK
                high, low = yh_ref[s, :, d:d + BLOCK], yl_ref[s, :, d:d + BLOCK]
                left = col_hi[b * BLOCK:(b + 1) * BLOCK, :]
                rest = col_lo[b * BLOCK:(b + 1) * BLOCK, :]
                total = total + (dot32(high, left) + (dot32(low, left) + dot32(high, rest)))
            for h in range(BLOCK // rows):
                for z in range(nz):
                    turned[s, a * (BLOCK // rows) + h, z] = total[
                        h * rows:(h + 1) * rows, z * width:(z + 1) * width
                    ]
        back[s, me] = turned[s, me]
        for k in range(1, peers):
            backward(s, k).start()

    @pl.loop(0, ns)
    def _(s):
        for k in range(1, peers):
            backward(s, k).wait_recv()
        remesh_rows(
            lambda z, r: jnp.concatenate(
                [back[s, p, z, pl.ds(r, step), :] for p in range(peers)], axis=1
            )
        )

        def store(c, total):
            for z in range(nz):
                out_ref[s, z, :, c:c + BLOCK] = total[z * rows:(z + 1) * rows]

        diffuse_rows(s, store)

    @pl.loop(0, ns)
    def _(s):
        for k in range(1, peers):
            forward(s, k).wait_send()
            backward(s, k).wait_send()


def sweeps_on_device(peers, scalars, velocity_x, velocity_y, shift_x, shift_y, schmidt):
    ns, nz, rows, nx = scalars.shape
    ny, width = rows * peers, nx // peers
    along_x = fetch_velocity(velocity_x)
    along_y = fetch_velocity(velocity_y)
    diffusivity = jnp.exp2((3 - schmidt).astype(jnp.float32))
    line_x = jnp.roll(response(0.5 * diffusivity, nx), -(REACH + 2), axis=1)
    line_y = response(diffusivity, ny)
    xh, xl = circulant_blocks(line_x)
    yh, yl = circulant_blocks(line_y)
    f32, bf16 = jnp.float32, jnp.bfloat16
    vmem = pl.BlockSpec(memory_space=pltpu.VMEM)
    dma = pltpu.SemaphoreType.DMA((ns, peers - 1))
    return pl.pallas_call(
        functools.partial(sweeps_kernel, peers),
        out_shape=jax.ShapeDtypeStruct(scalars.shape, f32),
        in_specs=[vmem] * 9,
        out_specs=vmem,
        scratch_shapes=[
            pltpu.VMEM((nz, 6, rows, nx), f32),
            pltpu.VMEM((nz, 6, rows, nx), f32),
            pltpu.VMEM((nz * rows, nx), bf16),
            pltpu.VMEM((nz * rows, nx), bf16),
            pltpu.VMEM((nz * rows, nx), f32),
            pltpu.VMEM((ny, nz * width), bf16),
            pltpu.VMEM((ny, nz * width), bf16),
            pltpu.VMEM((ny + 16, nz * width), f32),
            pltpu.VMEM((ns, peers, nz, rows + 8, width), f32),
            pltpu.VMEM((ns, peers, nz, rows + 8, width), f32),
            pltpu.VMEM((ns, peers, nz, rows, width), f32),
            pltpu.VMEM((ns, peers, nz, rows, width), f32),
            dma, dma, dma, dma,
        ],
        compiler_params=pltpu.CompilerParams(
            collective_id=0, has_side_effects=True, vmem_limit_bytes=62 * 2**20
        ),
    )(
        scalars, along_x, along_y, shift_x[:, :, None], shift_y[None, :], xh, xl, yh, yl
    )


def fits_kernel(mesh):
    return NY % mesh.shape["space"] == 0 and NY // mesh.shape["space"] in (128, 256)


def solution(mesh):
    peers = mesh.shape["space"]
    body = functools.partial(sweeps_on_device, peers) if fits_kernel(mesh) else on_device
    return jax.shard_map(
        body,
        mesh=mesh,
        in_specs=(
            P("scalar", None, "space", None),
            P(None, "space", "scalar"),
            P(None, "space", "scalar"),
            P(None, "space"),
            P("space"),
            P("scalar"),
        ),
        out_specs=P("scalar", None, "space", None),
        check_vma=False,
    )
```

```python
import functools
import math

import jax
import jax.numpy as jnp
import numpy as np
from jax import lax
from jax.experimental import pallas as pl
from jax.experimental.pallas import tpu as pltpu
from jax.sharding import PartitionSpec as P

NY = 1024


def spline(distance):
    magnitude = jnp.abs(distance)
    far_part = jnp.maximum(3.0 - magnitude, 0.0)
    middle = jnp.maximum(2.0 - magnitude, 0.0)
    near_part = jnp.maximum(1.0 - magnitude, 0.0)
    return (far_part**5 - 6.0 * middle**5 + 15.0 * near_part**5) / 120.0


def remesh(fields, fraction, shift_line):
    summed = jnp.zeros_like(fields)
    for offset in range(-2, 4):
        weight = spline(offset - fraction)
        summed = summed + jnp.roll(fields * weight, offset, axis=-1)
    line_shift = shift_line[None, :, :, None]
    moved = summed
    for amount in range(-8, 9):
        moved = jnp.where(line_shift == amount, jnp.roll(summed, amount, axis=-1), moved)
    return moved


def remesh_columns(fields, fraction, shift_cols):
    summed = jnp.zeros_like(fields)
    for offset in range(-2, 4):
        weight = spline(offset - fraction)
        summed = summed + jnp.roll(fields * weight[None], offset, axis=2)
    column_shift = shift_cols[None, None, None, :]
    moved = summed
    for amount in range(-8, 9):
        moved = jnp.where(column_shift == amount, jnp.roll(summed, amount, axis=2), moved)
    return moved


def spectral_tables(length):
    midpoint = length // 2
    column = jnp.arange(length, dtype=jnp.int32)
    wavenum = jnp.where(column <= midpoint, column, column - midpoint)
    phases = column[:, None] * wavenum[None, :] % length
    angles = phases.astype(jnp.float32) * (2.0 * math.pi / length)
    forward = jnp.where((column <= midpoint)[None, :], jnp.cos(angles), jnp.sin(angles))
    inverse_weight = jnp.where((wavenum == 0) | (column == midpoint), 1.0, 2.0) / length
    inverse = forward.T * inverse_weight[:, None]
    relative = wavenum.astype(jnp.float32) / midpoint
    return (forward, inverse, relative * relative)


def diffuse(fields, diffusivity, tables):
    forward, inverse, wave_square = tables
    initial = fields.shape
    rows_flat = fields.reshape(-1, initial[-1])
    spectra = jnp.dot(
        rows_flat, forward, precision=lax.Precision.HIGHEST, preferred_element_type=jnp.float32
    )
    damping = jnp.exp(-diffusivity[:, None] * wave_square[None, :])
    spectra = spectra.reshape(initial) * damping[:, None, None, :]
    result = jnp.dot(
        spectra.reshape(-1, initial[-1]),
        inverse,
        precision=lax.Precision.HIGHEST,
        preferred_element_type=jnp.float32,
    )
    return result.reshape(initial)


def diffuse_columns(fields, diffusivity, tables):
    forward, inverse, wave_square = tables
    spectra = jnp.einsum(
        "jk,szjx->szkx",
        forward,
        fields,
        precision=lax.Precision.HIGHEST,
        preferred_element_type=jnp.float32,
    )
    damping = jnp.exp(-diffusivity[:, None] * wave_square[None, :])
    spectra = spectra * damping[:, None, :, None]
    return jnp.einsum(
        "kj,szkx->szjx",
        inverse,
        spectra,
        precision=lax.Precision.HIGHEST,
        preferred_element_type=jnp.float32,
    )


def one_sweep(fields, fraction, shift_line, diffusivity, tables):
    return diffuse(remesh(fields, fraction, shift_line), diffusivity, tables)


def fetch_velocity(velocity_x):
    return lax.all_gather(velocity_x, "scalar", axis=2, tiled=True)


def on_device(scalars, velocity_x, velocity_y, shift_x, shift_y, schmidt):
    diffusivity = jnp.exp2((3 - schmidt).astype(jnp.float32))
    tables_x = spectral_tables(scalars.shape[3])
    tables_y = spectral_tables(NY)
    along_x = fetch_velocity(velocity_x)
    fields = one_sweep(scalars, along_x, shift_x, 0.5 * diffusivity, tables_x)
    along_y = lax.all_gather(velocity_y, "scalar", axis=2, tiled=True)
    fields_cols, velocity_cols = (
        lax.all_to_all(fields, "space", split_axis=3, concat_axis=2, tiled=True),
        lax.all_to_all(along_y[None], "space", split_axis=3, concat_axis=2, tiled=True),
    )
    remeshed = remesh_columns(fields_cols, velocity_cols[0], shift_y)
    returned = diffuse_columns(remeshed, diffusivity, tables_y)
    fields = lax.all_to_all(returned, "space", split_axis=2, concat_axis=3, tiled=True)
    along_x = fetch_velocity(velocity_x)
    return one_sweep(fields, along_x, shift_x, 0.5 * diffusivity, tables_x)


BLOCK = 256
REACH = 8
MESH = pl.DeviceIdType.MESH


def spline_weights(f):
    g = 1.0 - f

    def fifth(v):
        w = v * v
        return w * w * v

    f0, f1, f2 = fifth(f), fifth(1.0 + f), fifth(2.0 + f)
    g0, g1, g2 = fifth(g), fifth(1.0 + g), fifth(2.0 + g)
    c = 1.0 / 120.0
    return (
        g0 * c,
        (g1 - 6.0 * g0) * c,
        (g2 - 6.0 * g1 + 15.0 * g0) * c,
        (f2 - 6.0 * f1 + 15.0 * f0) * c,
        (f1 - 6.0 * f0) * c,
        f0 * c,
    )


def response(kappa, length):
    half = length // 2
    k = np.arange(half + 1)
    weight = np.where((k == 0) | (k == half), 1.0, 2.0) / length
    phase = (k[:, None] * np.arange(length)[None, :]) % length
    table = (np.cos(phase * (2.0 * np.pi / length)) * weight[:, None]).astype(np.float32)
    relative = jnp.arange(half + 1).astype(jnp.float32) / half
    damping = jnp.exp(-kappa[:, None] * relative * relative)
    return jnp.dot(damping, table, precision=lax.Precision.HIGHEST, preferred_element_type=jnp.float32)


def circulant_kernel(g_ref, hi_ref, lo_ref):
    length = g_ref.shape[-1]
    wide = jnp.broadcast_to(g_ref[0], (BLOCK, length))
    turned = pltpu.roll(wide, 0, 1, stride=1, stride_axis=0)
    high = turned.astype(jnp.bfloat16)
    hi_ref[0] = high
    lo_ref[0] = (turned - high.astype(jnp.float32)).astype(jnp.bfloat16)


def circulant_blocks(g):
    count, length = g.shape
    spec = pl.BlockSpec((1, BLOCK, length), lambda i: (i, 0, 0))
    return pl.pallas_call(
        circulant_kernel,
        grid=(count,),
        in_specs=[pl.BlockSpec((1, 1, length), lambda i: (i, 0, 0))],
        out_specs=[spec, spec],
        out_shape=[jax.ShapeDtypeStruct((count, BLOCK, length), jnp.bfloat16)] * 2,
    )(g[:, None, :])


def halves(v):
    high = v.astype(jnp.bfloat16)
    return high, (v - high.astype(jnp.float32)).astype(jnp.bfloat16)


def dot32(a, b):
    return jnp.dot(a, b, preferred_element_type=jnp.float32)


def sweeps_kernel(
    peers, groups,
    q_ref, vx_ref, vy_ref, sx_ref, sy_ref, xh_ref, xl_ref, yh_ref, yl_ref,
    out_ref,
    wx, wy, part_hi, part_lo, swept, col_hi, col_lo, tall,
    ext, cols, turned, back, held,
    sendv, recvv, send1, recv1, send2, recv2,
):
    ns, nz, rows, nx = q_ref.shape
    ny = rows * peers
    width = nx // peers
    me = lax.axis_index("space")
    bx, by = nx // BLOCK, ny // BLOCK

    barrier = pltpu.get_barrier_semaphore()
    for k in range(1, peers):
        pl.semaphore_signal(barrier, inc=1, device_id={"space": lax.rem(me + k, peers)}, device_id_type=MESH)
    mine = lax.axis_index("scalar")
    for k in range(1, groups):
        pl.semaphore_signal(barrier, inc=1, device_id={"scalar": lax.rem(mine + k, groups)}, device_id_type=MESH)
    pl.semaphore_wait(barrier, peers + groups - 2)

    def spread(n, k):
        return pltpu.make_async_remote_copy(
            src_ref=(vx_ref, vy_ref)[n], dst_ref=held.at[n, mine],
            send_sem=sendv.at[n, k - 1], recv_sem=recvv.at[n, k - 1],
            device_id={"scalar": lax.rem(mine + k, groups)}, device_id_type=MESH,
        )

    for n in range(2):
        for k in range(1, groups):
            spread(n, k).start()
    held[0, mine] = vx_ref[...]
    held[1, mine] = vy_ref[...]

    step = 16
    per = rows // step

    def weigh(n, w_ref):
        for k in range(1, groups):
            spread(n, k).wait_recv()

        @pl.loop(0, nz * per)
        def _(i):
            z, r = i // per, pl.multiple_of((i % per) * step, step)
            f = jnp.concatenate([held[n, g, z, pl.ds(r, step), :] for g in range(groups)], axis=1)
            for m, w in enumerate(spline_weights(f)):
                w_ref[z, m, pl.ds(r, step), :] = w

    weigh(0, wx)

    def remesh_rows(load):
        @pl.loop(0, nz * per, unroll=2)
        def _(i):
            z, r = i // per, pl.multiple_of((i % per) * step, step)
            q = load(z, r)
            acc = q * wx[z, 0, pl.ds(r, step), :]
            for m in range(1, 6):
                acc = acc + pltpu.roll(q * wx[z, m, pl.ds(r, step), :], m, 1)
            shift = sx_ref[z, pl.ds(r, step), :] + REACH
            for places, low in (((1, 2, 3), 3), ((4, 8, 12, 16), 28)):
                now, base = shift & low, acc
                for place in places:
                    acc = jnp.where(now == place, pltpu.roll(base, place, 1), acc)
            at = pl.multiple_of(z * rows + r, step)
            part_hi[pl.ds(at, step), :], part_lo[pl.ds(at, step), :] = halves(acc)

    def diffuse_rows(s, store):
        for b in range(bx):
            total = jnp.zeros((nz * rows, BLOCK), jnp.float32)
            for a in range(bx):
                d = ((b - a) % bx) * BLOCK
                high, low = xh_ref[s, :, d:d + BLOCK], xl_ref[s, :, d:d + BLOCK]
                left = part_hi[:, a * BLOCK:(a + 1) * BLOCK]
                rest = part_lo[:, a * BLOCK:(a + 1) * BLOCK]
                total = total + (dot32(left, high) + (dot32(left, low) + dot32(rest, high)))
            store(b * BLOCK, total)

    def forward(s, k):
        dest = lax.rem(me + k, peers)
        return pltpu.make_async_remote_copy(
            src_ref=ext.at[s, dest], dst_ref=cols.at[s, me],
            send_sem=send1.at[s, k - 1], recv_sem=recv1.at[s, k - 1],
            device_id={"space": dest}, device_id_type=MESH,
        )

    def backward(s, k):
        dest = lax.rem(me + k, peers)
        return pltpu.make_async_remote_copy(
            src_ref=turned.at[s, dest], dst_ref=back.at[s, me],
            send_sem=send2.at[s, k - 1], recv_sem=recv2.at[s, k - 1],
            device_id={"space": dest}, device_id_type=MESH,
        )

    edge = lax.broadcasted_iota(jnp.int32, (8, width), 0)

    def first(s, start):
        remesh_rows(lambda z, r: q_ref[s, z, pl.ds(r, step), :])

        def store(c, total):
            swept[:, c:c + BLOCK] = total

        diffuse_rows(s, store)
        if start:
            weigh(1, wy)

        @pl.loop(0, nz * peers)
        def _(i):
            p, z = i // nz, i % nz
            lanes = pl.ds(pl.multiple_of(p * width, width), width)
            y = swept[pl.ds(pl.multiple_of(z * rows, rows), rows), lanes]
            pad = jnp.zeros((8, width), jnp.float32)
            acc = jnp.zeros((rows + 16, width), jnp.float32)
            for m in range(-2, 4):
                term = jnp.concatenate([pad, y * wy[z, m + 2, :, lanes], pad], axis=0)
                acc = acc + (term if m == 0 else pltpu.roll(term, m % (rows + 16), 0))
            ext[s, p, z, 0:rows, :] = acc[8:8 + rows]
            ext[s, p, z, rows:rows + 8, :] = jnp.where(edge < 3, acc[rows + 8:], acc[:8])

        cols[s, me] = ext[s, me]

    @pl.loop(0, 1)
    def _(s):
        first(s, True)

    for k in range(1, peers):
        forward(0, k).start()

    @pl.loop(1, ns)
    def _(s):
        first(s, False)
        for k in range(1, peers):
            forward(s, k).start()

    @pl.loop(0, ns)
    def _(s):
        for k in range(1, peers):
            forward(s, k).wait_recv()

        for p in range(peers):
            for z in range(nz):
                lanes = slice(z * width, (z + 1) * width)
                top = jnp.where(edge < 3, cols[s, (p - 1) % peers, z, rows:rows + 8, :], 0.0)
                low = jnp.where(edge >= 6, cols[s, (p + 1) % peers, z, rows:rows + 8, :], 0.0)
                at = 8 + p * rows
                tall[at:at + 8, lanes] = cols[s, p, z, 0:8, :] + top
                tall[at + 8:at + rows - 8, lanes] = cols[s, p, z, 8:rows - 8, :]
                tall[at + rows - 8:at + rows, lanes] = cols[s, p, z, rows - 8:rows, :] + low
        tall[0:8, :] = tall[ny:ny + 8, :]
        tall[ny + 8:ny + 16, :] = tall[8:16, :]

        @pl.loop(0, peers)
        def _(p):
            at = pl.multiple_of(p * rows, rows)
            ahead = REACH - sy_ref[...]
            for z in range(nz):
                lanes = slice(z * width, (z + 1) * width)
                u = tall[pl.ds(at, rows + 16), lanes]
                for bit in (1, 2, 4, 8, 16):
                    u = jnp.where((ahead & bit) != 0, pltpu.roll(u, rows + 16 - bit, 0), u)
                col_hi[pl.ds(at, rows), lanes], col_lo[pl.ds(at, rows), lanes] = halves(u[:rows])

        for a in range(by):
            total = jnp.zeros((BLOCK, nz * width), jnp.float32)
            for b in range(by):
                d = ((b - a) % by) * BLOCK
                high, low = yh_ref[s, :, d:d + BLOCK], yl_ref[s, :, d:d + BLOCK]
                left = col_hi[b * BLOCK:(b + 1) * BLOCK, :]
                rest = col_lo[b * BLOCK:(b + 1) * BLOCK, :]
                total = total + (dot32(high, left) + (dot32(low, left) + dot32(high, rest)))
            for h in range(BLOCK // rows):
                for z in range(nz):
                    turned[s, a * (BLOCK // rows) + h, z] = total[
                        h * rows:(h + 1) * rows, z * width:(z + 1) * width
                    ]
        back[s, me] = turned[s, me]
        for k in range(1, peers):
            backward(s, k).start()

    @pl.loop(0, ns)
    def _(s):
        for k in range(1, peers):
            backward(s, k).wait_recv()
        remesh_rows(
            lambda z, r: jnp.concatenate(
                [back[s, p, z, pl.ds(r, step), :] for p in range(peers)], axis=1
            )
        )

        def store(c, total):
            for z in range(nz):
                out_ref[s, z, :, c:c + BLOCK] = total[z * rows:(z + 1) * rows]

        diffuse_rows(s, store)

    @pl.loop(0, ns)
    def _(s):
        for k in range(1, peers):
            forward(s, k).wait_send()
            backward(s, k).wait_send()

    for n in range(2):
        for k in range(1, groups):
            spread(n, k).wait_send()


def sweeps_on_device(peers, groups, scalars, velocity_x, velocity_y, shift_x, shift_y, schmidt):
    ns, nz, rows, nx = scalars.shape
    ny, width = rows * peers, nx // peers
    diffusivity = jnp.exp2((3 - schmidt).astype(jnp.float32))
    line_x = jnp.roll(response(0.5 * diffusivity, nx), -(REACH + 2), axis=1)
    line_y = response(diffusivity, ny)
    xh, xl = circulant_blocks(line_x)
    yh, yl = circulant_blocks(line_y)
    f32, bf16 = jnp.float32, jnp.bfloat16
    vmem = pl.BlockSpec(memory_space=pltpu.VMEM)
    dma = pltpu.SemaphoreType.DMA((ns, peers - 1))
    return pl.pallas_call(
        functools.partial(sweeps_kernel, peers, groups),
        out_shape=jax.ShapeDtypeStruct(scalars.shape, f32),
        in_specs=[vmem] * 9,
        out_specs=vmem,
        scratch_shapes=[
            pltpu.VMEM((nz, 6, rows, nx), f32),
            pltpu.VMEM((nz, 6, rows, nx), f32),
            pltpu.VMEM((nz * rows, nx), bf16),
            pltpu.VMEM((nz * rows, nx), bf16),
            pltpu.VMEM((nz * rows, nx), f32),
            pltpu.VMEM((ny, nz * width), bf16),
            pltpu.VMEM((ny, nz * width), bf16),
            pltpu.VMEM((ny + 16, nz * width), f32),
            pltpu.VMEM((ns, peers, nz, rows + 8, width), f32),
            pltpu.VMEM((ns, peers, nz, rows + 8, width), f32),
            pltpu.VMEM((ns, peers, nz, rows, width), f32),
            pltpu.VMEM((ns, peers, nz, rows, width), f32),
            pltpu.VMEM((2, groups) + velocity_x.shape, f32),
            pltpu.SemaphoreType.DMA((2, groups - 1)),
            pltpu.SemaphoreType.DMA((2, groups - 1)),
            dma, dma, dma, dma,
        ],
        compiler_params=pltpu.CompilerParams(
            collective_id=0, has_side_effects=True, vmem_limit_bytes=62 * 2**20
        ),
    )(
        scalars, velocity_x, velocity_y, shift_x[:, :, None], shift_y[None, :], xh, xl, yh, yl
    )


def fits_kernel(mesh):
    return NY % mesh.shape["space"] == 0 and NY // mesh.shape["space"] in (128, 256)


def solution(mesh):
    peers = mesh.shape["space"]
    body = functools.partial(sweeps_on_device, peers, mesh.shape["scalar"]) if fits_kernel(mesh) else on_device
    return jax.shard_map(
        body,
        mesh=mesh,
        in_specs=(
            P("scalar", None, "space", None),
            P(None, "space", "scalar"),
            P(None, "space", "scalar"),
            P(None, "space"),
            P("space"),
            P("scalar"),
        ),
        out_specs=P("scalar", None, "space", None),
        check_vma=False,
    )
```
